256 devices in a mesh: stn: 64 (over z_lo, y, x), tm: 4 (over z_hi, core).
Axes of the slice: x: 4, y: 4, z: 8 (z_hi: 2, z_lo: 4; z = z_hi * 4 + z_lo), core: 2. Of those that a mesh axis runs over, the one named last changes fastest.
Arguments:
- voltages: bfloat16 [2, 8, 1024, 12288], P(None, None, 'stn', 'tm'), may hold values from -6 to 6
- filter_taps: float32 [12, 32], replicated, may hold values from -1.75 to 1.75
Outputs:
- visibilities: float32 [256, 2, 1024, 1024], P(('stn', 'tm'))
The draws below stay inside these ranges and needn't reach their ends.
All inputs are finite; a program needn't handle non-finite values.
Results may differ from the reference program's by a relative error of at most 0.0035.
Values may be sent and summed in bfloat16 or wider, within the bound.
A program may use at most 192 MiB of HBM per device.

```python
import math
import jax
import jax.numpy as jnp
from jax import lax

INPUTS = 1024
FINE = 32
TAPS = 12
COARSE = 8
SPECTRA = 384
SAMPLES = 12288
PAIRS = 256


def block_scale(stream_key, shape, cuts, smallest, largest):
    def one(position, parts):
        draws = jax.random.uniform(jax.random.fold_in(jax.random.fold_in(stream_key, 6), position), (parts,), jnp.float32, smallest / len(cuts), largest / len(cuts))
        return jnp.repeat(jnp.exp(draws), shape[position] // parts).reshape((-1,) + (1,) * (len(shape) - position - 1))

    factor_of = one(*cuts[0])
    for cut in cuts[1:]:
        factor_of = factor_of * one(*cut)
    return factor_of


def scatter_about(key, extent, spread, limit, pieces=(), held_as=jnp.bfloat16):
    gain = block_scale(key, extent, pieces, -0.22, 0.18) if pieces else 1.0
    values = jax.random.normal(key, extent, jnp.float32) * spread * gain
    return jnp.minimum(jnp.maximum(values, -limit), limit).astype(held_as)


def setup_inputs(seed: int = 0) -> dict:
    seeds = jax.random.split(jax.random.key(seed), 3)
    return {
        "voltages": scatter_about(seeds[0], (2, COARSE, INPUTS, SAMPLES), 1.0, 6.0, ((2, 64), (3, 4))),
        "filter_taps": scatter_about(seeds[1], (TAPS, FINE), TAPS ** -0.5, 1.75, (), jnp.float32),
    }


def dft_matrix(fine_len):
    steps_k = jnp.arange(fine_len)
    angle = 2.0 * math.pi / fine_len * (steps_k[:, None] * steps_k[None, :] % fine_len).astype(jnp.float32)
    cosine = jnp.cos(angle)
    sine = jnp.sin(angle)
    upper = jnp.concatenate([cosine, -sine], axis=1)
    lower = jnp.concatenate([sine, cosine], axis=1)
    return jnp.concatenate([upper, lower], axis=0) / jnp.sqrt(jnp.float32(fine_len))

def spectra_of(extended, filter_taps, spec_count):
    comp_count, coarse, inputs, _ = extended.shape
    tap_count, fine_len = filter_taps.shape
    segments = extended.reshape(comp_count, coarse, inputs, spec_count + tap_count - 1, fine_len).astype(jnp.float32)
    filtered = segments[:, :, :, 0:spec_count, :] * filter_taps[0]
    for tap_idx in range(1, tap_count):
        filtered = filtered + segments[:, :, :, tap_idx:tap_idx + spec_count, :] * filter_taps[tap_idx]
    stacked = jnp.concatenate([filtered[0], filtered[1]], axis=-1)
    turned = jnp.dot(stacked, dft_matrix(fine_len), precision=lax.Precision.HIGHEST)
    turned = turned.reshape(coarse, inputs, spec_count, 2, fine_len).astype(jnp.bfloat16)
    return jnp.transpose(turned, (0, 4, 3, 1, 2))

def correlate(pair_data, factor):
    inputs = pair_data.shape[1]
    stacked = pair_data.reshape(2 * inputs, pair_data.shape[2]).astype(jnp.float32)
    gram_matrix = jnp.dot(stacked, stacked.T, precision=lax.Precision.HIGHEST)
    vis_re = (gram_matrix[:inputs, :inputs] + gram_matrix[inputs:, inputs:]) * factor
    vis_im = (gram_matrix[inputs:, :inputs] - gram_matrix[:inputs, inputs:]) * factor
    return jnp.stack([vis_re, vis_im], axis=0)

def reference(voltages, filter_taps):
    padded = jnp.pad(voltages, ((0, 0), (0, 0), (0, 0), (0, (TAPS - 1) * FINE)))
    by_channel = jnp.transpose(padded, (1, 0, 2, 3))
    factor = 1.0 / SPECTRA

    def one_channel(channel_data):
        spectra = spectra_of(channel_data[:, None], filter_taps, SPECTRA)[0]
        return lax.map(lambda pair_data: correlate(pair_data, factor), spectra)
    result = lax.map(one_channel, by_channel)
    return result.reshape(PAIRS, 2, INPUTS, INPUTS)
```

```python
import functools
import math

import jax
import jax.numpy as jnp
import numpy as np
from jax import lax
from jax.experimental import pallas as pl
from jax.experimental.pallas import tpu as pltpu
from jax.sharding import PartitionSpec as P

MESH = pl.DeviceIdType.MESH

COARSE = 8
INPUTS = 16
FINE = 32
TAPS = 12
FRAMES = 96
HALF = FINE // 2
BLOCK = 8
WINDOW = 640
BLOCKS = 2 * FRAMES // BLOCK
GROUPS = BLOCKS // 8
OWN = FRAMES * FINE
RIM = 384
ALL = 2 * OWN
K = 2 * WINDOW
CHUNK = 2 * 2 * FRAMES


def dft_columns():
    k = np.arange(FINE)[:, None]
    lane = np.arange(256)[None, :]
    out = np.zeros((2, 2, FINE, 256), np.float64)
    comp = (lane // 64) % 2
    for parity in range(2):
        fine = 2 * ((lane // 128) * 8 + (lane // 8) % 8) + parity
        angle = 2.0 * math.pi / FINE * (fine * k % FINE)
        out[parity, 0] = np.where(comp == 0, np.cos(angle), -np.sin(angle))
        out[parity, 1] = np.where(comp == 0, np.sin(angle), np.cos(angle))
    return (out / math.sqrt(FINE)).astype(np.float32)


def swap_groups(rows):
    rows = list(rows)
    lane = lax.broadcasted_iota(jnp.int32, rows[0].shape, 1)
    for bit in range(3):
        step = 8 << bit
        low = (lane // step) % 2 == 0
        for a in range(8):
            if a >> bit & 1:
                continue
            b = a | 1 << bit
            left, right = rows[a], rows[b]
            rows[a] = jnp.where(low, left, pltpu.roll(right, step, 1))
            rows[b] = jnp.where(low, pltpu.roll(left, 128 - step, 1), right)
    return rows


def exchange_kernel(
    volts, taps, dft, owned,
    vbuf, sbuf, w_hi, w_lo,
    load_sem, sib_send, sib_recv, rim_send, rim_recv, send_sem, recv_sem, own_sem, b_ready, bb_ready,
):
    s = lax.axis_index("stn")
    t = lax.axis_index("tm")
    zl = s // 16
    y = s // 4 % 4
    zh = t // 2
    c = t % 2
    sibling = (s, zh * 2 + 1 - c)
    barrier = pltpu.get_barrier_semaphore()

    def coarse_at(k):
        return (zl + k // 2) % 4 * 2 + (y // 2 + k) % 2

    def own_load(coarse):
        return pltpu.make_async_copy(
            volts.at[:, coarse],
            vbuf.at[:, coarse, :, pl.ds(pl.multiple_of(c * OWN, 128), OWN)],
            load_sem.at[coarse],
        )

    def to_sibling(coarse):
        return pltpu.make_async_remote_copy(
            volts.at[:, coarse],
            vbuf.at[:, coarse, :, pl.ds(pl.multiple_of(c * OWN, 128), OWN)],
            sib_send,
            sib_recv.at[coarse],
            device_id=sibling,
            device_id_type=MESH,
        )

    rim_at = pl.ds(ALL, RIM)

    pl.semaphore_signal(barrier, 1, device_id=sibling, device_id_type=MESH)

    @pl.when(zh == 0)
    def _():
        @pl.loop(0, 64)
        def _(i):
            pl.semaphore_signal(barrier, 1, device_id=((s + i) % 64, 2 + c), device_id_type=MESH)

    @pl.loop(0, COARSE)
    def _(k):
        own_load(coarse_at(k)).start()

    pl.semaphore_wait(barrier, 1 + 64 * zh)

    @pl.when(jnp.logical_and(zh == 1, c == 0))
    def _():
        @pl.loop(0, COARSE)
        def _(k):
            coarse = coarse_at(k)
            pltpu.make_async_remote_copy(
                volts.at[:, coarse, :, pl.ds(0, RIM)],
                vbuf.at[:, coarse, :, rim_at],
                rim_send,
                rim_recv.at[coarse],
                device_id=(s, 0),
                device_id_type=MESH,
            ).start()

    @pl.loop(0, COARSE)
    def _(k):
        to_sibling(coarse_at(k)).start()

    @pl.when(zh == 1)
    def _():
        @pl.loop(0, 64)
        def _(i):
            pl.semaphore_signal(b_ready, 1, device_id=((s + i) % 64, c), device_id_type=MESH)

        vbuf[:, :, :, rim_at] = jnp.zeros((2, COARSE, INPUTS, RIM), jnp.bfloat16)

    frame = lax.broadcasted_iota(jnp.int32, (FINE, 128), 1) % BLOCK
    spread = [jnp.broadcast_to(taps[:, i : i + 1], (FINE, 128)) for i in range(TAPS)]
    for seg in range(WINDOW // FINE):
        tap_of = jnp.zeros((FINE, 128), jnp.float32)
        for q in range(BLOCK):
            if 0 <= seg - q < TAPS:
                tap_of = jnp.where(frame == q, spread[seg - q], tap_of)
        for comp in range(2):
            for half in range(2):
                weight = tap_of * dft[c, comp, :, half * 128 : half * 128 + 128]
                high = weight.astype(jnp.bfloat16)
                at = (pl.ds(comp * WINDOW + seg * FINE, FINE), pl.ds(half * 128, 128))
                w_hi[at] = high
                w_lo[at] = (weight - high.astype(jnp.float32)).astype(jnp.bfloat16)

    def spectra(coarse, group):
        rows = []
        for j in range(8 * group, 8 * group + 8):
            at = pl.ds(j * BLOCK * FINE, WINDOW)
            rows.append(jnp.concatenate([vbuf[0, coarse, :, at], vbuf[1, coarse, :, at]], axis=1))
        left = jnp.concatenate(rows, axis=0)
        both = jnp.dot(left, w_hi[...], preferred_element_type=jnp.float32)
        both = both + jnp.dot(left, w_lo[...], preferred_element_type=jnp.float32)
        for half in range(2):
            turned = swap_groups(
                [both[16 * j : 16 * j + 16, 128 * half : 128 * half + 128] for j in range(8)]
            )
            for fine in range(8):
                sbuf[coarse, half * 8 + fine, :, pl.ds(group * 128, 128)] = turned[fine].astype(jnp.bfloat16)

    def send(coarse, place, to_zh):
        to_s = coarse * 8 + place
        mine = jnp.logical_and(to_s == s, to_zh == zh)
        source = sbuf.at[coarse, 2 * place + to_zh]

        @pl.when(jnp.logical_not(mine))
        def _():
            pltpu.make_async_remote_copy(
                source, owned.at[zh * 64 + s], send_sem, recv_sem,
                device_id=(to_s, to_zh * 2 + c), device_id_type=MESH,
            ).start()

        @pl.when(mine)
        def _():
            pltpu.make_async_copy(source, owned.at[zh * 64 + s], own_sem).start()

    @pl.loop(0, COARSE)
    def _(k):
        coarse = coarse_at(k)
        own_load(coarse).wait()
        to_sibling(coarse).wait_recv()
        spectra(coarse, 0)
        spectra(coarse, 1)

        @pl.when(zh == 1)
        def _():
            spectra(coarse, 2)

            @pl.loop(0, 8)
            def _(place):
                send(coarse, place, 0)

    @pl.when(zh == 0)
    def _():
        pl.semaphore_wait(b_ready, 64)
        pl.semaphore_signal(bb_ready, 1, device_id=(s, 2 + c), device_id_type=MESH)

        @pl.loop(0, COARSE)
        def _(k):
            coarse = coarse_at(k)
            rim_here = vbuf.at[:, coarse, :, rim_at]
            pltpu.make_async_copy(rim_here, rim_here, rim_recv.at[coarse]).wait()

            @pl.when(c == 0)
            def _():
                pltpu.make_async_remote_copy(
                    rim_here, rim_here, rim_send, rim_recv.at[coarse],
                    device_id=(s, 1), device_id_type=MESH,
                ).start()

            spectra(coarse, 2)

            @pl.loop(0, 16)
            def _(place):
                send(coarse, place // 2, place % 2)

    @pl.when(zh == 1)
    def _():
        pl.semaphore_wait(bb_ready, 1)

        @pl.loop(0, COARSE)
        def _(k):
            @pl.loop(0, 8)
            def _(place):
                send(coarse_at(k), place, 1)

    pltpu.make_async_copy(volts, volts, sib_send).wait()

    @pl.when(c == 0)
    def _():
        rim_all = vbuf.at[:, :, :, rim_at]
        pltpu.make_async_copy(rim_all, rim_all, rim_send).wait()

    pltpu.make_async_copy(sbuf.at[0, 0], sbuf.at[0, 0], own_sem).wait()
    sent = owned.at[pl.ds(0, 127)]
    pltpu.make_async_copy(sent, sent, send_sem).wait()
    pltpu.make_async_copy(sent, sent, recv_sem).wait()


def exchange(voltages, taps):
    vmem = pl.BlockSpec(memory_space=pltpu.VMEM)
    return pl.pallas_call(
        exchange_kernel,
        out_shape=jax.ShapeDtypeStruct((128, INPUTS, CHUNK), jnp.bfloat16),
        in_specs=[pl.BlockSpec(memory_space=pl.ANY), vmem, vmem],
        out_specs=vmem,
        scratch_shapes=[
            pltpu.VMEM((2, COARSE, INPUTS, ALL + RIM), jnp.bfloat16),
            pltpu.VMEM((COARSE, HALF, INPUTS, CHUNK), jnp.bfloat16),
            pltpu.VMEM((K, 256), jnp.bfloat16),
            pltpu.VMEM((K, 256), jnp.bfloat16),
            pltpu.SemaphoreType.DMA((COARSE,)),
            pltpu.SemaphoreType.DMA,
            pltpu.SemaphoreType.DMA((COARSE,)),
            pltpu.SemaphoreType.DMA,
            pltpu.SemaphoreType.DMA((COARSE,)),
            pltpu.SemaphoreType.DMA,
            pltpu.SemaphoreType.DMA,
            pltpu.SemaphoreType.DMA,
            pltpu.SemaphoreType.REGULAR,
            pltpu.SemaphoreType.REGULAR,
        ],
        compiler_params=pltpu.CompilerParams(
            collective_id=0, has_side_effects=True, vmem_limit_bytes=32 << 20
        ),
        name="exchange",
    )(voltages, taps, jnp.asarray(dft_columns()))


def gram_kernel(factor, data, out):
    i = pl.program_id(0)
    rows = out.shape[1]
    re = jnp.zeros((rows, 1024), jnp.float32)
    im = jnp.zeros((rows, 1024), jnp.float32)
    lane = lax.broadcasted_iota(jnp.int32, (rows, 128), 1)
    sign = jnp.where(lane < 64, 1.0, -1.0)
    at = pl.ds(pl.multiple_of(i * rows, rows), rows)
    dims = (((1,), (1,)), ((), ()))
    for zh in range(2):
        left = data[zh, at, :]
        turned = []
        for tile in range(3):
            part = left[:, tile * 128 : tile * 128 + 128].astype(jnp.float32)
            turned.append((pltpu.roll(part, 64, 1) * sign).astype(jnp.bfloat16))
        turned = jnp.concatenate(turned, axis=1)
        right = data[zh]
        re = re + lax.dot_general(left, right, dims, preferred_element_type=jnp.float32)
        im = im + lax.dot_general(turned, right, dims, preferred_element_type=jnp.float32)
    out[0] = re * factor
    out[1] = im * factor


def gram(data, factor):
    rows = 128
    return pl.pallas_call(
        functools.partial(gram_kernel, factor),
        out_shape=jax.ShapeDtypeStruct((2, 1024, 1024), jnp.float32),
        grid=(1024 // rows,),
        in_specs=[pl.BlockSpec((2, 1024, CHUNK), lambda i: (0, 0, 0))],
        out_specs=pl.BlockSpec((2, rows, 1024), lambda i: (0, i, 0)),
        compiler_params=pltpu.CompilerParams(vmem_limit_bytes=32 << 20),
        name="gram",
    )(data)


def on_device(voltages, filter_taps):
    owned = exchange(voltages, filter_taps.T)
    return gram(owned.reshape(2, 1024, CHUNK), 1.0 / (4 * FRAMES))[None]


def solution(mesh):
    return jax.shard_map(
        on_device,
        mesh=mesh,
        in_specs=(P(None, None, "stn", "tm"), P()),
        out_specs=P(("stn", "tm"), None, None, None),
        check_vma=False,
    )
```

```python
import functools
import math

import jax
import jax.numpy as jnp
from jax import lax
from jax.experimental import pallas as pl
from jax.experimental.pallas import tpu as pltpu
from jax.sharding import PartitionSpec as P

MESH = pl.DeviceIdType.MESH

COARSE = 8
INPUTS = 16
FINE = 32
TAPS = 12
FRAMES = 96
HALF = FINE // 2
BLOCK = 8
WINDOW = 640
BLOCKS = 2 * FRAMES // BLOCK
GROUPS = BLOCKS // 8
OWN = FRAMES * FINE
RIM = 384
ALL = 2 * OWN
K = 2 * WINDOW
CHUNK = 2 * 2 * FRAMES
LAG = 4
COLUMNS = 256
VMEM_LIMIT = 52 << 20


COSINES = [round(math.cos(math.pi * i / 16), 15) / math.sqrt(FINE) for i in range(17)]


def dft_columns(parity, comp, half):
    row = lax.broadcasted_iota(jnp.int32, (FINE, 128), 0)
    lane = lax.broadcasted_iota(jnp.int32, (FINE, 128), 1)
    fine = 2 * (half * 8 + lane // 8 % 8) + parity
    out = lane // 64
    turn = (fine * row + 8 * (out - comp)) & 31
    turn = jnp.minimum(turn, 32 - turn)
    value = jnp.zeros((FINE, 128), jnp.float32)
    for step in range(17):
        value = jnp.where(turn == step, COSINES[step], value)
    return value


def swap_groups(rows):
    rows = list(rows)
    lane = lax.broadcasted_iota(jnp.int32, rows[0].shape, 1)
    for bit in range(3):
        step = 8 << bit
        low = (lane // step) % 2 == 0
        for a in range(8):
            if a >> bit & 1:
                continue
            b = a | 1 << bit
            left, right = rows[a], rows[b]
            rows[a] = jnp.where(low, left, pltpu.roll(right, step, 1))
            rows[b] = jnp.where(low, pltpu.roll(left, 128 - step, 1), right)
    return rows


def exchange_kernel(
    volts, taps, owned,
    vbuf, sbuf, w_hi, w_lo,
    load_sem, sib_send, sib_recv, rim_send, rim_recv, send_sem, recv_sem, own_sem, b_ready, bb_ready,
):
    s = lax.axis_index("stn")
    t = lax.axis_index("tm")
    zl = s // 16
    y = s // 4 % 4
    zh = t // 2
    c = t % 2
    sibling = (s, zh * 2 + 1 - c)
    barrier = pltpu.get_barrier_semaphore()

    def coarse_at(k):
        return (zl + k // 2) % 4 * 2 + (y // 2 + k) % 2

    def own_load(coarse):
        return pltpu.make_async_copy(
            volts.at[:, coarse],
            vbuf.at[:, coarse, :, pl.ds(pl.multiple_of(c * OWN, 128), OWN)],
            load_sem.at[coarse],
        )

    def to_sibling(coarse):
        return pltpu.make_async_remote_copy(
            volts.at[:, coarse],
            vbuf.at[:, coarse, :, pl.ds(pl.multiple_of(c * OWN, 128), OWN)],
            sib_send,
            sib_recv.at[coarse],
            device_id=sibling,
            device_id_type=MESH,
        )

    rim_at = pl.ds(ALL, RIM)

    pl.semaphore_signal(barrier, 1, device_id=sibling, device_id_type=MESH)

    @pl.when(zh == 0)
    def _():
        @pl.loop(1, 64)
        def _(i):
            pl.semaphore_signal(barrier, 1, device_id=((s + i) % 64, c), device_id_type=MESH)

    @pl.loop(0, COARSE)
    def _(k):
        own_load(coarse_at(k)).start()

    @pl.when(zh == 0)
    def _():
        @pl.loop(0, 64)
        def _(i):
            pl.semaphore_signal(barrier, 1, device_id=((s + i) % 64, 2 + c), device_id_type=MESH)

    @pl.when(zh == 1)
    def _():
        vbuf[:, :, :, rim_at] = jnp.zeros((2, COARSE, INPUTS, RIM), jnp.bfloat16)

    eye = lax.broadcasted_iota(jnp.int32, (FINE, FINE), 0) == lax.broadcasted_iota(jnp.int32, (FINE, FINE), 1)
    turned_taps = lax.dot_general(
        eye.astype(jnp.float32), taps[...], (((1,), (1,)), ((), ())),
        precision=lax.Precision.HIGHEST, preferred_element_type=jnp.float32,
    )
    frame = lax.broadcasted_iota(jnp.int32, (FINE, 128), 1) % BLOCK
    spread = [jnp.broadcast_to(turned_taps[:, i : i + 1], (FINE, 128)) for i in range(TAPS)]
    columns = [[dft_columns(c, comp, half) for half in range(2)] for comp in range(2)]
    for seg in range(WINDOW // FINE):
        tap_of = jnp.zeros((FINE, 128), jnp.float32)
        for q in range(BLOCK):
            if 0 <= seg - q < TAPS:
                tap_of = jnp.where(frame == q, spread[seg - q], tap_of)
        for comp in range(2):
            for half in range(2):
                weight = tap_of * columns[comp][half]
                high = weight.astype(jnp.bfloat16)
                at = (pl.ds(comp * WINDOW + seg * FINE, FINE), pl.ds(half * 128, 128))
                w_hi[at] = high
                w_lo[at] = (weight - high.astype(jnp.float32)).astype(jnp.bfloat16)

    def starts(tile):
        if tile < 2:
            base = (c if tile == 0 else 1 - c) * OWN
            return [base + j * BLOCK * FINE for j in range(8)]
        return [core * OWN + j * BLOCK * FINE for core in range(2) for j in range(8, 12)]

    def spectra(coarse, tiles):
        rows = []
        for tile in tiles:
            for start in starts(tile):
                at = pl.ds(pl.multiple_of(start, 128), WINDOW)
                rows.append(jnp.concatenate([vbuf[0, coarse, :, at], vbuf[1, coarse, :, at]], axis=1))
        left = jnp.concatenate(rows, axis=0)
        both = jnp.dot(left, w_hi[...], preferred_element_type=jnp.float32)
        both = both + jnp.dot(left, w_lo[...], preferred_element_type=jnp.float32)
        for i, tile in enumerate(tiles):
            for half in range(2):
                turned = swap_groups(
                    [
                        both[16 * j : 16 * j + 16, 128 * half : 128 * half + 128]
                        for j in range(8 * i, 8 * i + 8)
                    ]
                )
                for fine in range(8):
                    sbuf[coarse, half * 8 + fine, :, pl.ds(tile * 128, 128)] = turned[fine].astype(
                        jnp.bfloat16
                    )

    def send(coarse, place, to_zh, lo, size):
        to_s = coarse * 8 + place
        mine = jnp.logical_and(to_s == s, to_zh == zh)
        part = pl.ds(lo, size)
        source = sbuf.at[coarse, 2 * place + to_zh, :, part]
        target = owned.at[zh * 64 + s, :, part]

        @pl.when(jnp.logical_not(mine))
        def _():
            pltpu.make_async_remote_copy(
                source, target, send_sem, recv_sem,
                device_id=(to_s, to_zh * 2 + c), device_id_type=MESH,
            ).start()

        @pl.when(mine)
        def _():
            pltpu.make_async_copy(source, target, own_sem).start()

    def send_first(coarse, to_zh):
        @pl.loop(0, 8)
        def _(place):
            send(coarse, place, to_zh, 0, 128)

    def start_siblings():
        @pl.loop(0, COARSE)
        def _(k):
            to_sibling(coarse_at(k)).start()

    def first(k):
        coarse = coarse_at(k)
        own_load(coarse).wait()
        spectra(coarse, (0,))

    @pl.when(zh == 0)
    def _():
        @pl.loop(0, LAG)
        def _(k):
            first(k)

    pl.semaphore_wait(barrier, 64 + zh)

    @pl.when(jnp.logical_and(zh == 1, c == 0))
    def _():
        @pl.loop(0, COARSE)
        def _(k):
            coarse = coarse_at(k)
            pltpu.make_async_remote_copy(
                volts.at[:, coarse, :, pl.ds(0, RIM)],
                vbuf.at[:, coarse, :, rim_at],
                rim_send,
                rim_recv.at[coarse],
                device_id=(s, 0),
                device_id_type=MESH,
            ).start()

    start_siblings()

    @pl.when(zh == 0)
    def _():
        @pl.loop(0, COARSE)
        def _(k):
            send_first(coarse_at(k), 0)

            @pl.when(k + LAG < COARSE)
            def _():
                first(k + LAG)

        @pl.loop(0, COARSE)
        def _(k):
            coarse = coarse_at(k)
            pl.semaphore_wait(b_ready.at[coarse], 8)
            pl.semaphore_signal(bb_ready.at[coarse], 1, device_id=(s, 2 + c), device_id_type=MESH)
            send_first(coarse, 1)

    @pl.when(zh == 1)
    def _():
        @pl.loop(0, 64)
        def _(i):
            pl.semaphore_signal(
                b_ready.at[s // 8], 1, device_id=((s + i) % 64, c), device_id_type=MESH
            )

        @pl.loop(0, COARSE)
        def _(k):
            first(k)
            send_first(coarse_at(k), 0)

        @pl.loop(0, COARSE)
        def _(k):
            coarse = coarse_at(k)
            pl.semaphore_wait(bb_ready.at[coarse], 1)
            send_first(coarse, 1)

    @pl.loop(0, COARSE)
    def _(k):
        coarse = coarse_at(k)
        to_sibling(coarse).wait_recv()

        @pl.when(zh == 0)
        def _():
            rim_here = vbuf.at[:, coarse, :, rim_at]
            pltpu.make_async_copy(rim_here, rim_here, rim_recv.at[coarse]).wait()

            @pl.when(c == 0)
            def _():
                pltpu.make_async_remote_copy(
                    rim_here, rim_here, rim_send, rim_recv.at[coarse],
                    device_id=(s, 1), device_id_type=MESH,
                ).start()

        spectra(coarse, (1, 2))

        @pl.loop(0, 16)
        def _(place):
            send(coarse, place // 2, place % 2, 128, 256)

    pltpu.make_async_copy(volts, volts, sib_send).wait()

    @pl.when(c == 0)
    def _():
        rim_all = vbuf.at[:, :, :, rim_at]
        pltpu.make_async_copy(rim_all, rim_all, rim_send).wait()

    pltpu.make_async_copy(sbuf.at[0, 0], sbuf.at[0, 0], own_sem).wait()
    sent = owned.at[pl.ds(0, 127)]
    pltpu.make_async_copy(sent, sent, send_sem).wait()
    pltpu.make_async_copy(sent, sent, recv_sem).wait()


def exchange(voltages, taps):
    vmem = pl.BlockSpec(memory_space=pltpu.VMEM)
    return pl.pallas_call(
        exchange_kernel,
        out_shape=jax.ShapeDtypeStruct((128, INPUTS, CHUNK), jnp.bfloat16),
        in_specs=[pl.BlockSpec(memory_space=pl.ANY), vmem],
        out_specs=vmem,
        scratch_shapes=[
            pltpu.VMEM((2, COARSE, INPUTS, ALL + RIM), jnp.bfloat16),
            pltpu.VMEM((COARSE, HALF, INPUTS, CHUNK), jnp.bfloat16),
            pltpu.VMEM((K, 256), jnp.bfloat16),
            pltpu.VMEM((K, 256), jnp.bfloat16),
            pltpu.SemaphoreType.DMA((COARSE,)),
            pltpu.SemaphoreType.DMA,
            pltpu.SemaphoreType.DMA((COARSE,)),
            pltpu.SemaphoreType.DMA,
            pltpu.SemaphoreType.DMA((COARSE,)),
            pltpu.SemaphoreType.DMA,
            pltpu.SemaphoreType.DMA,
            pltpu.SemaphoreType.DMA,
            pltpu.SemaphoreType.REGULAR((COARSE,)),
            pltpu.SemaphoreType.REGULAR((COARSE,)),
        ],
        compiler_params=pltpu.CompilerParams(
            collective_id=0, has_side_effects=True, vmem_limit_bytes=VMEM_LIMIT
        ),
        name="exchange",
    )(voltages, taps)


def gram_kernel(factor, data, out, buf, sems):
    lane = lax.broadcasted_iota(jnp.int32, (COLUMNS, 128), 1)
    sign = jnp.where(lane < 64, -1.0, 1.0)
    left = jnp.concatenate([data[0], data[1]], axis=1)
    copies = []
    for i in range(1024 // COLUMNS):
        at = pl.ds(i * COLUMNS, COLUMNS)
        plain, turned = [], []
        for zh in range(2):
            plain.append(data[zh, at, :])
            for tile in range(CHUNK // 128):
                part = data[zh, at, pl.ds(tile * 128, 128)].astype(jnp.float32)
                turned.append((pltpu.roll(part, 64, 1) * sign).astype(jnp.bfloat16))
        right = jnp.concatenate(
            [jnp.concatenate(plain, axis=1), jnp.concatenate(turned, axis=1)], axis=0
        )
        both = lax.dot_general(
            left, right, (((1,), (1,)), ((), ())), preferred_element_type=jnp.float32
        )
        slot = i % 2
        if i >= 2:
            copies[i - 2].wait()
        buf[slot, 0] = both[:, :COLUMNS] * factor
        buf[slot, 1] = both[:, COLUMNS:] * factor
        copies.append(pltpu.make_async_copy(buf.at[slot], out.at[:, :, at], sems.at[slot]))
        copies[i].start()
    copies[-2].wait()
    copies[-1].wait()


def gram(data, factor):
    return pl.pallas_call(
        functools.partial(gram_kernel, factor),
        out_shape=jax.ShapeDtypeStruct((2, 1024, 1024), jnp.float32),
        in_specs=[pl.BlockSpec(memory_space=pltpu.VMEM)],
        out_specs=pl.BlockSpec(memory_space=pl.ANY),
        scratch_shapes=[
            pltpu.VMEM((2, 2, 1024, COLUMNS), jnp.float32),
            pltpu.SemaphoreType.DMA((2,)),
        ],
        compiler_params=pltpu.CompilerParams(vmem_limit_bytes=48 << 20),
        name="gram",
    )(data)


def on_device(voltages, filter_taps):
    owned = exchange(voltages, filter_taps)
    return gram(owned.reshape(2, 1024, CHUNK), 1.0 / (4 * FRAMES))[None]


def solution(mesh):
    return jax.shard_map(
        on_device,
        mesh=mesh,
        in_specs=(P(None, None, "stn", "tm"), P()),
        out_specs=P(("stn", "tm"), None, None, None),
        check_vma=False,
    )
```

```python
import functools
import math

import jax
import jax.numpy as jnp
from jax import lax
from jax.experimental import pallas as pl
from jax.experimental.pallas import tpu as pltpu
from jax.sharding import PartitionSpec as P

MESH = pl.DeviceIdType.MESH

COARSE = 8
INPUTS = 16
FINE = 32
TAPS = 12
FRAMES = 96
HALF = FINE // 2
BLOCK = 8
WINDOW = 640
BLOCKS = 2 * FRAMES // BLOCK
GROUPS = BLOCKS // 8
OWN = FRAMES * FINE
RIM = 384
ALL = 2 * OWN
K = 2 * WINDOW
CHUNK = 2 * 2 * FRAMES
COLUMNS = 256
VMEM_LIMIT = 52 << 20


COSINES = [round(math.cos(math.pi * i / 16), 15) / math.sqrt(FINE) for i in range(17)]


def dft_columns(parity, comp, half):
    row = lax.broadcasted_iota(jnp.int32, (FINE, 128), 0)
    lane = lax.broadcasted_iota(jnp.int32, (FINE, 128), 1)
    fine = 2 * (half * 8 + lane // 8 % 8) + parity
    out = lane // 64
    turn = (fine * row + 8 * (out - comp)) & 31
    turn = jnp.minimum(turn, 32 - turn)
    value = jnp.zeros((FINE, 128), jnp.float32)
    for step in range(17):
        value = jnp.where(turn == step, COSINES[step], value)
    return value


def swap_groups(rows):
    rows = list(rows)
    lane = lax.broadcasted_iota(jnp.int32, rows[0].shape, 1)
    for bit in range(3):
        step = 8 << bit
        low = (lane // step) % 2 == 0
        for a in range(8):
            if a >> bit & 1:
                continue
            b = a | 1 << bit
            left, right = rows[a], rows[b]
            rows[a] = jnp.where(low, left, pltpu.roll(right, step, 1))
            rows[b] = jnp.where(low, pltpu.roll(left, 128 - step, 1), right)
    return rows


def exchange_kernel(
    volts, taps, owned,
    vbuf, sbuf, w_hi, w_lo,
    load_sem, sib_send, sib_recv, rim_send, rim_recv, send_sem, recv_sem, own_sem, b_in, a_ready, b_ready, bb_ready,
):
    s = lax.axis_index("stn")
    t = lax.axis_index("tm")
    zl = s // 16
    y = s // 4 % 4
    zh = t // 2
    c = t % 2
    sibling = (s, zh * 2 + 1 - c)
    opposite = (s, 2 - 2 * zh + c)
    barrier = pltpu.get_barrier_semaphore()

    def coarse_at(k):
        return (zl + k // 2) % 4 * 2 + (y // 2 + k) % 2

    def own_load(coarse):
        return pltpu.make_async_copy(
            volts.at[:, coarse],
            vbuf.at[:, coarse, :, pl.ds(pl.multiple_of(c * OWN, 128), OWN)],
            load_sem.at[coarse],
        )

    def to_sibling(coarse):
        return pltpu.make_async_remote_copy(
            volts.at[:, coarse],
            vbuf.at[:, coarse, :, pl.ds(pl.multiple_of(c * OWN, 128), OWN)],
            sib_send,
            sib_recv.at[coarse],
            device_id=sibling,
            device_id_type=MESH,
        )

    rim_at = pl.ds(ALL, RIM)

    pl.semaphore_signal(barrier, 1, device_id=sibling, device_id_type=MESH)

    @pl.when(zh == 0)
    def _():
        pl.semaphore_signal(barrier, 1, device_id=opposite, device_id_type=MESH)

        @pl.loop(1, 64, unroll=9)
        def _(i):
            pl.semaphore_signal(barrier, 1, device_id=((s + i) % 64, c), device_id_type=MESH)

    @pl.loop(0, COARSE)
    def _(k):
        own_load(coarse_at(k)).start()

    def start_siblings():
        @pl.loop(0, COARSE)
        def _(k):
            to_sibling(coarse_at(k)).start()

    @pl.when(zh == 1)
    def _():
        pl.semaphore_wait(barrier, 2)
        pl.semaphore_signal(b_in, 1, device_id=opposite, device_id_type=MESH)

        @pl.when(c == 0)
        def _():
            @pl.loop(0, COARSE)
            def _(k):
                coarse = coarse_at(k)
                pltpu.make_async_remote_copy(
                    volts.at[:, coarse, :, pl.ds(0, RIM)],
                    vbuf.at[:, coarse, :, rim_at],
                    rim_send,
                    rim_recv.at[coarse],
                    device_id=(s, 0),
                    device_id_type=MESH,
                ).start()

        start_siblings()
        vbuf[:, :, :, rim_at] = jnp.zeros((2, COARSE, INPUTS, RIM), jnp.bfloat16)

    eye = lax.broadcasted_iota(jnp.int32, (FINE, FINE), 0) == lax.broadcasted_iota(jnp.int32, (FINE, FINE), 1)
    turned_taps = lax.dot_general(
        eye.astype(jnp.float32), taps[...], (((1,), (1,)), ((), ())),
        precision=lax.Precision.HIGHEST, preferred_element_type=jnp.float32,
    )
    frame = lax.broadcasted_iota(jnp.int32, (FINE, 128), 1) % BLOCK
    spread = [jnp.broadcast_to(turned_taps[:, i : i + 1], (FINE, 128)) for i in range(TAPS)]
    columns = [[dft_columns(c, comp, half) for half in range(2)] for comp in range(2)]
    for seg in range(WINDOW // FINE):
        tap_of = jnp.zeros((FINE, 128), jnp.float32)
        for q in range(BLOCK):
            if 0 <= seg - q < TAPS:
                tap_of = jnp.where(frame == q, spread[seg - q], tap_of)
        for comp in range(2):
            for half in range(2):
                weight = tap_of * columns[comp][half]
                high = weight.astype(jnp.bfloat16)
                at = (pl.ds(comp * WINDOW + seg * FINE, FINE), pl.ds(half * 128, 128))
                w_hi[at] = high
                w_lo[at] = (weight - high.astype(jnp.float32)).astype(jnp.bfloat16)

    def starts(tile):
        if tile < 2:
            base = (c if tile == 0 else 1 - c) * OWN
            return [base + j * BLOCK * FINE for j in range(8)]
        return [core * OWN + j * BLOCK * FINE for core in range(2) for j in range(8, 12)]

    def spectra(coarses, tiles):
        rows = []
        for coarse in coarses:
            for tile in tiles:
                for start in starts(tile):
                    at = pl.ds(pl.multiple_of(start, 128), WINDOW)
                    rows.append(
                        jnp.concatenate([vbuf[0, coarse, :, at], vbuf[1, coarse, :, at]], axis=1)
                    )
        left = jnp.concatenate(rows, axis=0)
        both = jnp.dot(left, w_hi[...], preferred_element_type=jnp.float32)
        both = both + jnp.dot(left, w_lo[...], preferred_element_type=jnp.float32)
        row = 0
        for coarse in coarses:
            for tile in tiles:
                for half in range(2):
                    turned = swap_groups(
                        [
                            both[row + 16 * j : row + 16 * j + 16, 128 * half : 128 * half + 128]
                            for j in range(8)
                        ]
                    )
                    for fine in range(8):
                        sbuf[coarse, half * 8 + fine, :, pl.ds(tile * 128, 128)] = turned[fine].astype(
                            jnp.bfloat16
                        )
                row += 128

    def send(coarse, place, to_zh, lo, size):
        to_s = coarse * 8 + place
        mine = jnp.logical_and(to_s == s, to_zh == zh)
        part = pl.ds(lo, size)
        source = sbuf.at[coarse, 2 * place + to_zh, :, part]
        target = owned.at[zh * 64 + s, :, part]

        @pl.when(jnp.logical_not(mine))
        def _():
            pltpu.make_async_remote_copy(
                source, target, send_sem, recv_sem,
                device_id=(to_s, to_zh * 2 + c), device_id_type=MESH,
            ).start()

        @pl.when(mine)
        def _():
            pltpu.make_async_copy(source, target, own_sem).start()

    def send_first(coarse, to_zh):
        @pl.loop(0, 8, unroll=8)
        def _(place):
            send(coarse, place, to_zh, 0, 128)

    def first(part):
        coarses = [coarse_at(4 * part + i) for i in range(4)]
        for coarse in coarses:
            own_load(coarse).wait()
        spectra(coarses, (0,))

    first(0)

    @pl.when(zh == 0)
    def _():
        pl.semaphore_wait(barrier, 64)
        start_siblings()
        pl.semaphore_wait(b_in, 1)
        pl.semaphore_signal(a_ready, 1, device_id=opposite, device_id_type=MESH)
        pl.semaphore_signal(b_ready.at[s // 8], 1)

        @pl.loop(1, 64, unroll=9)
        def _(i):
            pl.semaphore_signal(
                b_ready.at[s // 8], 1, device_id=((s + i) % 64, c), device_id_type=MESH
            )

    @pl.when(zh == 1)
    def _():
        pl.semaphore_wait(a_ready, 1)

    @pl.loop(0, 4)
    def _(k):
        send_first(coarse_at(k), 0)

    first(1)

    @pl.loop(4, COARSE)
    def _(k):
        send_first(coarse_at(k), 0)

    @pl.loop(0, COARSE)
    def _(k):
        coarse = coarse_at(k)

        @pl.when(zh == 0)
        def _():
            pl.semaphore_wait(b_ready.at[coarse], 8)
            pl.semaphore_signal(bb_ready.at[coarse], 1, device_id=(s, 2 + c), device_id_type=MESH)

        @pl.when(zh == 1)
        def _():
            pl.semaphore_wait(bb_ready.at[coarse], 1)

        send_first(coarse, 1)

    @pl.loop(0, COARSE // 2)
    def _(pair):
        coarses = [coarse_at(2 * pair), coarse_at(2 * pair + 1)]
        for coarse in coarses:
            to_sibling(coarse).wait_recv()

            @pl.when(zh == 0)
            def _():
                rim_here = vbuf.at[:, coarse, :, rim_at]
                pltpu.make_async_copy(rim_here, rim_here, rim_recv.at[coarse]).wait()

                @pl.when(c == 0)
                def _():
                    pltpu.make_async_remote_copy(
                        rim_here, rim_here, rim_send, rim_recv.at[coarse],
                        device_id=(s, 1), device_id_type=MESH,
                    ).start()

        spectra(coarses, (1, 2))

        for coarse in coarses:
            @pl.loop(0, 16, unroll=8)
            def _(place):
                send(coarse, place // 2, place % 2, 128, 256)

    pltpu.make_async_copy(volts, volts, sib_send).wait()

    @pl.when(c == 0)
    def _():
        rim_all = vbuf.at[:, :, :, rim_at]
        pltpu.make_async_copy(rim_all, rim_all, rim_send).wait()

    pltpu.make_async_copy(sbuf.at[0, 0], sbuf.at[0, 0], own_sem).wait()
    sent = owned.at[pl.ds(0, 127)]
    pltpu.make_async_copy(sent, sent, send_sem).wait()
    pltpu.make_async_copy(sent, sent, recv_sem).wait()


def exchange(voltages, taps):
    vmem = pl.BlockSpec(memory_space=pltpu.VMEM)
    return pl.pallas_call(
        exchange_kernel,
        out_shape=jax.ShapeDtypeStruct((128, INPUTS, CHUNK), jnp.bfloat16),
        in_specs=[pl.BlockSpec(memory_space=pl.ANY), vmem],
        out_specs=vmem,
        scratch_shapes=[
            pltpu.VMEM((2, COARSE, INPUTS, ALL + RIM), jnp.bfloat16),
            pltpu.VMEM((COARSE, HALF, INPUTS, CHUNK), jnp.bfloat16),
            pltpu.VMEM((K, 256), jnp.bfloat16),
            pltpu.VMEM((K, 256), jnp.bfloat16),
            pltpu.SemaphoreType.DMA((COARSE,)),
            pltpu.SemaphoreType.DMA,
            pltpu.SemaphoreType.DMA((COARSE,)),
            pltpu.SemaphoreType.DMA,
            pltpu.SemaphoreType.DMA((COARSE,)),
            pltpu.SemaphoreType.DMA,
            pltpu.SemaphoreType.DMA,
            pltpu.SemaphoreType.DMA,
            pltpu.SemaphoreType.REGULAR,
            pltpu.SemaphoreType.REGULAR,
            pltpu.SemaphoreType.REGULAR((COARSE,)),
            pltpu.SemaphoreType.REGULAR((COARSE,)),
        ],
        compiler_params=pltpu.CompilerParams(
            collective_id=0, has_side_effects=True, vmem_limit_bytes=VMEM_LIMIT
        ),
        name="exchange",
    )(voltages, taps)


def gram_kernel(factor, data, out, buf, sems):
    lane = lax.broadcasted_iota(jnp.int32, (COLUMNS, 128), 1)
    sign = jnp.where(lane < 64, -1.0, 1.0)
    left = jnp.concatenate([data[0], data[1]], axis=1)
    copies = []
    for i in range(1024 // COLUMNS):
        at = pl.ds(i * COLUMNS, COLUMNS)
        plain, turned = [], []
        for zh in range(2):
            plain.append(data[zh, at, :])
            for tile in range(CHUNK // 128):
                part = data[zh, at, pl.ds(tile * 128, 128)].astype(jnp.float32)
                turned.append((pltpu.roll(part, 64, 1) * sign).astype(jnp.bfloat16))
        right = jnp.concatenate(
            [jnp.concatenate(plain, axis=1), jnp.concatenate(turned, axis=1)], axis=0
        )
        both = lax.dot_general(
            left, right, (((1,), (1,)), ((), ())), preferred_element_type=jnp.float32
        )
        slot = i % 2
        if i >= 2:
            copies[i - 2].wait()
        buf[slot, 0] = both[:, :COLUMNS] * factor
        buf[slot, 1] = both[:, COLUMNS:] * factor
        copies.append(pltpu.make_async_copy(buf.at[slot], out.at[:, :, at], sems.at[slot]))
        copies[i].start()
    copies[-2].wait()
    copies[-1].wait()


def gram(data, factor):
    return pl.pallas_call(
        functools.partial(gram_kernel, factor),
        out_shape=jax.ShapeDtypeStruct((2, 1024, 1024), jnp.float32),
        in_specs=[pl.BlockSpec(memory_space=pltpu.VMEM)],
        out_specs=pl.BlockSpec(memory_space=pl.ANY),
        scratch_shapes=[
            pltpu.VMEM((2, 2, 1024, COLUMNS), jnp.float32),
            pltpu.SemaphoreType.DMA((2,)),
        ],
        compiler_params=pltpu.CompilerParams(vmem_limit_bytes=48 << 20),
        name="gram",
    )(data)


def on_device(voltages, filter_taps):
    owned = exchange(voltages, filter_taps)
    return gram(owned.reshape(2, 1024, CHUNK), 1.0 / (4 * FRAMES))[None]


def solution(mesh):
    return jax.shard_map(
        on_device,
        mesh=mesh,
        in_specs=(P(None, None, "stn", "tm"), P()),
        out_specs=P(("stn", "tm"), None, None, None),
        check_vma=False,
    )
```

```python
import functools
import math

import jax
import jax.numpy as jnp
from jax import lax
from jax.experimental import pallas as pl
from jax.experimental.pallas import tpu as pltpu
from jax.sharding import PartitionSpec as P

MESH = pl.DeviceIdType.MESH

COARSE = 8
INPUTS = 16
FINE = 32
TAPS = 12
FRAMES = 96
HALF = FINE // 2
BLOCK = 8
WINDOW = 640
BLOCKS = 2 * FRAMES // BLOCK
GROUPS = BLOCKS // 8
OWN = FRAMES * FINE
RIM = 384
ALL = 2 * OWN
K = 2 * WINDOW
CHUNK = 2 * 2 * FRAMES
COLUMNS = 256
VMEM_LIMIT = 52 << 20


COSINES = [round(math.cos(math.pi * i / 16), 15) / math.sqrt(FINE) for i in range(17)]


def dft_columns(parity, comp, half):
    row = lax.broadcasted_iota(jnp.int32, (FINE, 128), 0)
    lane = lax.broadcasted_iota(jnp.int32, (FINE, 128), 1)
    fine = 2 * (half * 8 + lane // 8 % 8) + parity
    out = lane // 64
    turn = (fine * row + 8 * (out - comp)) & 31
    turn = jnp.minimum(turn, 32 - turn)
    value = jnp.zeros((FINE, 128), jnp.float32)
    for step in range(17):
        value = jnp.where(turn == step, COSINES[step], value)
    return value


def swap_groups(rows):
    rows = list(rows)
    lane = lax.broadcasted_iota(jnp.int32, rows[0].shape, 1)
    for bit in range(3):
        step = 8 << bit
        low = (lane // step) % 2 == 0
        for a in range(8):
            if a >> bit & 1:
                continue
            b = a | 1 << bit
            left, right = rows[a], rows[b]
            rows[a] = jnp.where(low, left, pltpu.roll(right, step, 1))
            rows[b] = jnp.where(low, pltpu.roll(left, 128 - step, 1), right)
    return rows


def exchange_kernel(
    volts, taps, owned,
    vbuf, sbuf, w_hi, w_lo,
    load_sem, sib_send, sib_recv, rim_send, rim_recv, send_sem, recv_sem, own_sem, b_in, a_ready, b_ready, bb_ready,
):
    s = lax.axis_index("stn")
    t = lax.axis_index("tm")
    zl = s // 16
    y = s // 4 % 4
    zh = t // 2
    c = t % 2
    sibling = (s, zh * 2 + 1 - c)
    opposite = (s, 2 - 2 * zh + c)
    barrier = pltpu.get_barrier_semaphore()

    def coarse_at(k):
        return (zl + k // 2) % 4 * 2 + (y // 2 + k) % 2

    def own_load(coarse):
        return pltpu.make_async_copy(
            volts.at[:, coarse],
            vbuf.at[:, coarse, :, pl.ds(pl.multiple_of(c * OWN, 128), OWN)],
            load_sem.at[coarse],
        )

    def to_sibling(coarse):
        return pltpu.make_async_remote_copy(
            volts.at[:, coarse],
            vbuf.at[:, coarse, :, pl.ds(pl.multiple_of(c * OWN, 128), OWN)],
            sib_send,
            sib_recv.at[coarse],
            device_id=sibling,
            device_id_type=MESH,
        )

    rim_at = pl.ds(ALL, RIM)

    pl.semaphore_signal(barrier, 1, device_id=sibling, device_id_type=MESH)

    @pl.when(zh == 0)
    def _():
        pl.semaphore_signal(barrier, 1, device_id=opposite, device_id_type=MESH)

        @pl.loop(1, 64, unroll=9)
        def _(i):
            pl.semaphore_signal(barrier, 1, device_id=((s + i) % 64, c), device_id_type=MESH)

    @pl.loop(0, COARSE)
    def _(k):
        own_load(coarse_at(k)).start()

    def start_siblings():
        @pl.loop(0, COARSE)
        def _(k):
            to_sibling(coarse_at(k)).start()

    @pl.when(zh == 1)
    def _():
        pl.semaphore_wait(barrier, 2)
        pl.semaphore_signal(b_in, 1, device_id=opposite, device_id_type=MESH)

        @pl.when(c == 0)
        def _():
            @pl.loop(0, COARSE)
            def _(k):
                coarse = coarse_at(k)
                pltpu.make_async_remote_copy(
                    volts.at[:, coarse, :, pl.ds(0, RIM)],
                    vbuf.at[:, coarse, :, rim_at],
                    rim_send,
                    rim_recv.at[coarse],
                    device_id=(s, 0),
                    device_id_type=MESH,
                ).start()

        start_siblings()
        vbuf[:, :, :, rim_at] = jnp.zeros((2, COARSE, INPUTS, RIM), jnp.bfloat16)

    eye = lax.broadcasted_iota(jnp.int32, (FINE, FINE), 0) == lax.broadcasted_iota(jnp.int32, (FINE, FINE), 1)
    turned_taps = lax.dot_general(
        eye.astype(jnp.float32), taps[...], (((1,), (1,)), ((), ())),
        precision=lax.Precision.HIGHEST, preferred_element_type=jnp.float32,
    )
    frame = lax.broadcasted_iota(jnp.int32, (FINE, 128), 1) % BLOCK
    spread = [jnp.broadcast_to(turned_taps[:, i : i + 1], (FINE, 128)) for i in range(TAPS)]
    columns = [[dft_columns(c, comp, half) for half in range(2)] for comp in range(2)]
    for seg in range(WINDOW // FINE):
        tap_of = jnp.zeros((FINE, 128), jnp.float32)
        for q in range(BLOCK):
            if 0 <= seg - q < TAPS:
                tap_of = jnp.where(frame == q, spread[seg - q], tap_of)
        for comp in range(2):
            for half in range(2):
                weight = tap_of * columns[comp][half]
                high = weight.astype(jnp.bfloat16)
                at = (pl.ds(comp * WINDOW + seg * FINE, FINE), pl.ds(half * 128, 128))
                w_hi[at] = high
                w_lo[at] = (weight - high.astype(jnp.float32)).astype(jnp.bfloat16)

    def starts(tile):
        if tile < 2:
            base = (c if tile == 0 else 1 - c) * OWN
            return [base + j * BLOCK * FINE for j in range(8)]
        return [core * OWN + j * BLOCK * FINE for core in range(2) for j in range(8, 12)]

    def spectra(coarses, tiles):
        rows = []
        for coarse in coarses:
            for tile in tiles:
                for start in starts(tile):
                    at = pl.ds(pl.multiple_of(start, 128), WINDOW)
                    rows.append(
                        jnp.concatenate([vbuf[0, coarse, :, at], vbuf[1, coarse, :, at]], axis=1)
                    )
        left = jnp.concatenate(rows, axis=0)
        both = jnp.dot(left, w_hi[...], preferred_element_type=jnp.float32)
        both = both + jnp.dot(left, w_lo[...], preferred_element_type=jnp.float32)
        row = 0
        for coarse in coarses:
            for tile in tiles:
                for half in range(2):
                    turned = swap_groups(
                        [
                            both[row + 16 * j : row + 16 * j + 16, 128 * half : 128 * half + 128]
                            for j in range(8)
                        ]
                    )
                    for fine in range(8):
                        sbuf[coarse, half * 8 + fine, :, pl.ds(tile * 128, 128)] = turned[fine].astype(
                            jnp.bfloat16
                        )
                row += 128

    def send(coarse, place, to_zh, lo, size):
        to_s = coarse * 8 + place
        mine = jnp.logical_and(to_s == s, to_zh == zh)
        part = pl.ds(lo, size)
        source = sbuf.at[coarse, 2 * place + to_zh, :, part]
        target = owned.at[zh * 64 + s, :, part]

        @pl.when(jnp.logical_not(mine))
        def _():
            pltpu.make_async_remote_copy(
                source, target, send_sem, recv_sem,
                device_id=(to_s, to_zh * 2 + c), device_id_type=MESH,
            ).start()

        @pl.when(mine)
        def _():
            pltpu.make_async_copy(source, target, own_sem).start()

    def send_first(coarse, to_zh):
        @pl.loop(0, 8, unroll=8)
        def _(place):
            send(coarse, place, to_zh, 0, 128)

    def first(part):
        coarses = [coarse_at(4 * part + i) for i in range(4)]
        for coarse in coarses:
            own_load(coarse).wait()
        spectra(coarses, (0,))

    first(0)

    @pl.when(zh == 0)
    def _():
        pl.semaphore_wait(barrier, 64)
        start_siblings()
        pl.semaphore_wait(b_in, 1)
        pl.semaphore_signal(a_ready, 1, device_id=opposite, device_id_type=MESH)
        pl.semaphore_signal(b_ready.at[s // 8], 1)

        @pl.loop(1, 64, unroll=9)
        def _(i):
            pl.semaphore_signal(
                b_ready.at[s // 8], 1, device_id=((s + i) % 64, c), device_id_type=MESH
            )

    @pl.when(zh == 1)
    def _():
        pl.semaphore_wait(a_ready, 1)

    @pl.loop(0, 4)
    def _(k):
        send_first(coarse_at(k), 0)

    first(1)

    @pl.loop(4, COARSE)
    def _(k):
        send_first(coarse_at(k), 0)

    @pl.loop(0, COARSE)
    def _(k):
        coarse = coarse_at(k)

        @pl.when(zh == 0)
        def _():
            pl.semaphore_wait(b_ready.at[coarse], 8)
            pl.semaphore_signal(bb_ready.at[coarse], 1, device_id=(s, 2 + c), device_id_type=MESH)

        @pl.when(zh == 1)
        def _():
            pl.semaphore_wait(bb_ready.at[coarse], 1)

        send_first(coarse, 1)

    @pl.loop(0, COARSE // 2)
    def _(pair):
        coarses = [coarse_at(2 * pair), coarse_at(2 * pair + 1)]
        for coarse in coarses:
            to_sibling(coarse).wait_recv()

            @pl.when(zh == 0)
            def _():
                rim_here = vbuf.at[:, coarse, :, rim_at]
                pltpu.make_async_copy(rim_here, rim_here, rim_recv.at[coarse]).wait()

                @pl.when(c == 0)
                def _():
                    pltpu.make_async_remote_copy(
                        rim_here, rim_here, rim_send, rim_recv.at[coarse],
                        device_id=(s, 1), device_id_type=MESH,
                    ).start()

        spectra(coarses, (1, 2))

        for coarse in coarses:
            @pl.loop(0, 8, unroll=8)
            def _(place):
                send(coarse, place, 0, 128, 256)

    @pl.loop(0, COARSE)
    def _(k):
        coarse = coarse_at(k)

        @pl.loop(0, 8, unroll=8)
        def _(place):
            send(coarse, place, 1, 128, 256)

    pltpu.make_async_copy(volts, volts, sib_send).wait()

    @pl.when(c == 0)
    def _():
        rim_all = vbuf.at[:, :, :, rim_at]
        pltpu.make_async_copy(rim_all, rim_all, rim_send).wait()

    pltpu.make_async_copy(sbuf.at[0, 0], sbuf.at[0, 0], own_sem).wait()
    sent = owned.at[pl.ds(0, 127)]
    pltpu.make_async_copy(sent, sent, send_sem).wait()
    pltpu.make_async_copy(sent, sent, recv_sem).wait()


def exchange(voltages, taps):
    vmem = pl.BlockSpec(memory_space=pltpu.VMEM)
    return pl.pallas_call(
        exchange_kernel,
        out_shape=jax.ShapeDtypeStruct((128, INPUTS, CHUNK), jnp.bfloat16),
        in_specs=[pl.BlockSpec(memory_space=pl.ANY), vmem],
        out_specs=vmem,
        scratch_shapes=[
            pltpu.VMEM((2, COARSE, INPUTS, ALL + RIM), jnp.bfloat16),
            pltpu.VMEM((COARSE, HALF, INPUTS, CHUNK), jnp.bfloat16),
            pltpu.VMEM((K, 256), jnp.bfloat16),
            pltpu.VMEM((K, 256), jnp.bfloat16),
            pltpu.SemaphoreType.DMA((COARSE,)),
            pltpu.SemaphoreType.DMA,
            pltpu.SemaphoreType.DMA((COARSE,)),
            pltpu.SemaphoreType.DMA,
            pltpu.SemaphoreType.DMA((COARSE,)),
            pltpu.SemaphoreType.DMA,
            pltpu.SemaphoreType.DMA,
            pltpu.SemaphoreType.DMA,
            pltpu.SemaphoreType.REGULAR,
            pltpu.SemaphoreType.REGULAR,
            pltpu.SemaphoreType.REGULAR((COARSE,)),
            pltpu.SemaphoreType.REGULAR((COARSE,)),
        ],
        compiler_params=pltpu.CompilerParams(
            collective_id=0, has_side_effects=True, vmem_limit_bytes=VMEM_LIMIT
        ),
        name="exchange",
    )(voltages, taps)


def gram_kernel(factor, data, out, buf, sems):
    lane = lax.broadcasted_iota(jnp.int32, (COLUMNS, 128), 1)
    sign = jnp.where(lane < 64, -1.0, 1.0)
    left = jnp.concatenate([data[0], data[1]], axis=1)
    copies = []
    for i in range(1024 // COLUMNS):
        at = pl.ds(i * COLUMNS, COLUMNS)
        plain, turned = [], []
        for zh in range(2):
            plain.append(data[zh, at, :])
            for tile in range(CHUNK // 128):
                part = data[zh, at, pl.ds(tile * 128, 128)].astype(jnp.float32)
                turned.append((pltpu.roll(part, 64, 1) * sign).astype(jnp.bfloat16))
        right = jnp.concatenate(
            [jnp.concatenate(plain, axis=1), jnp.concatenate(turned, axis=1)], axis=0
        )
        both = lax.dot_general(
            left, right, (((1,), (1,)), ((), ())), preferred_element_type=jnp.float32
        )
        buf[i, 0] = both[:, :COLUMNS] * factor
        buf[i, 1] = both[:, COLUMNS:] * factor
        copies.append(pltpu.make_async_copy(buf.at[i], out.at[:, :, at], sems.at[i]))
        copies[i].start()
    for copy in copies:
        copy.wait()


def gram(data, factor):
    return pl.pallas_call(
        functools.partial(gram_kernel, factor),
        out_shape=jax.ShapeDtypeStruct((2, 1024, 1024), jnp.float32),
        in_specs=[pl.BlockSpec(memory_space=pltpu.VMEM)],
        out_specs=pl.BlockSpec(memory_space=pl.ANY),
        scratch_shapes=[
            pltpu.VMEM((1024 // COLUMNS, 2, 1024, COLUMNS), jnp.float32),
            pltpu.SemaphoreType.DMA((1024 // COLUMNS,)),
        ],
        compiler_params=pltpu.CompilerParams(vmem_limit_bytes=48 << 20),
        name="gram",
    )(data)


def on_device(voltages, filter_taps):
    owned = exchange(voltages, filter_taps)
    return gram(owned.reshape(2, 1024, CHUNK), 1.0 / (4 * FRAMES))[None]


def solution(mesh):
    return jax.shard_map(
        on_device,
        mesh=mesh,
        in_specs=(P(None, None, "stn", "tm"), P()),
        out_specs=P(("stn", "tm"), None, None, None),
        check_vma=False,
    )
```

```python
import functools
import math

import jax
import jax.numpy as jnp
from jax import lax
from jax.experimental import pallas as pl
from jax.experimental.pallas import tpu as pltpu
from jax.sharding import PartitionSpec as P

MESH = pl.DeviceIdType.MESH

COARSE = 8
INPUTS = 16
FINE = 32
TAPS = 12
FRAMES = 96
HALF = FINE // 2
BLOCK = 8
WINDOW = 640
BLOCKS = 2 * FRAMES // BLOCK
GROUPS = BLOCKS // 8
OWN = FRAMES * FINE
RIM = 384
ALL = 2 * OWN
K = 2 * WINDOW
CHUNK = 2 * 2 * FRAMES
COLUMNS = 256
VMEM_LIMIT = 52 << 20


COSINES = [round(math.cos(math.pi * i / 16), 15) / math.sqrt(FINE) for i in range(17)]


def dft_columns(parity, comp, half):
    row = lax.broadcasted_iota(jnp.int32, (FINE, 128), 0)
    lane = lax.broadcasted_iota(jnp.int32, (FINE, 128), 1)
    fine = 2 * (half * 8 + lane // 8 % 8) + parity
    out = lane // 64
    turn = (fine * row + 8 * (out - comp)) & 31
    turn = jnp.minimum(turn, 32 - turn)
    value = jnp.zeros((FINE, 128), jnp.float32)
    for step in range(17):
        value = jnp.where(turn == step, COSINES[step], value)
    return value


def swap_groups(rows):
    rows = list(rows)
    lane = lax.broadcasted_iota(jnp.int32, rows[0].shape, 1)
    for bit in range(3):
        step = 8 << bit
        low = (lane // step) % 2 == 0
        for a in range(8):
            if a >> bit & 1:
                continue
            b = a | 1 << bit
            left, right = rows[a], rows[b]
            rows[a] = jnp.where(low, left, pltpu.roll(right, step, 1))
            rows[b] = jnp.where(low, pltpu.roll(left, 128 - step, 1), right)
    return rows


def exchange_kernel(
    volts, taps, owned,
    vbuf, sbuf, w_hi, w_lo,
    load_sem, sib_send, sib_recv, rim_send, rim_recv, send_sem, recv_sem, own_sem, b_in, a_ready, b_ready, bb_ready,
):
    s = lax.axis_index("stn")
    t = lax.axis_index("tm")
    zl = s // 16
    y = s // 4 % 4
    zh = t // 2
    c = t % 2
    sibling = (s, zh * 2 + 1 - c)
    opposite = (s, 2 - 2 * zh + c)
    barrier = pltpu.get_barrier_semaphore()

    def coarse_at(k):
        ahead = jnp.where(zh == 0, k // 2, 4 - k // 2)
        return (zl + ahead) % 4 * 2 + (y // 2 + k) % 2

    def own_load(coarse):
        return pltpu.make_async_copy(
            volts.at[:, coarse],
            vbuf.at[:, coarse, :, pl.ds(pl.multiple_of(c * OWN, 128), OWN)],
            load_sem.at[coarse],
        )

    def to_sibling(coarse):
        return pltpu.make_async_remote_copy(
            volts.at[:, coarse],
            vbuf.at[:, coarse, :, pl.ds(pl.multiple_of(c * OWN, 128), OWN)],
            sib_send,
            sib_recv.at[coarse],
            device_id=sibling,
            device_id_type=MESH,
        )

    rim_at = pl.ds(ALL, RIM)

    pl.semaphore_signal(barrier, 1, device_id=sibling, device_id_type=MESH)

    @pl.when(zh == 0)
    def _():
        pl.semaphore_signal(barrier, 1, device_id=opposite, device_id_type=MESH)

        @pl.loop(1, 64, unroll=9)
        def _(i):
            pl.semaphore_signal(barrier, 1, device_id=((s + i) % 64, c), device_id_type=MESH)

    @pl.loop(0, COARSE)
    def _(k):
        own_load(coarse_at(k)).start()

    def start_siblings():
        @pl.loop(0, COARSE)
        def _(k):
            to_sibling(coarse_at(k)).start()

    @pl.when(zh == 1)
    def _():
        pl.semaphore_wait(barrier, 2)
        pl.semaphore_signal(b_in, 1, device_id=opposite, device_id_type=MESH)

        @pl.when(c == 0)
        def _():
            @pl.loop(0, COARSE)
            def _(k):
                coarse = coarse_at(k)
                pltpu.make_async_remote_copy(
                    volts.at[:, coarse, :, pl.ds(0, RIM)],
                    vbuf.at[:, coarse, :, rim_at],
                    rim_send,
                    rim_recv.at[coarse],
                    device_id=(s, 0),
                    device_id_type=MESH,
                ).start()

        start_siblings()
        vbuf[:, :, :, rim_at] = jnp.zeros((2, COARSE, INPUTS, RIM), jnp.bfloat16)

    eye = lax.broadcasted_iota(jnp.int32, (FINE, FINE), 0) == lax.broadcasted_iota(jnp.int32, (FINE, FINE), 1)
    turned_taps = lax.dot_general(
        eye.astype(jnp.float32), taps[...], (((1,), (1,)), ((), ())),
        precision=lax.Precision.HIGHEST, preferred_element_type=jnp.float32,
    )
    frame = lax.broadcasted_iota(jnp.int32, (FINE, 128), 1) % BLOCK
    spread = [jnp.broadcast_to(turned_taps[:, i : i + 1], (FINE, 128)) for i in range(TAPS)]
    columns = [[dft_columns(c, comp, half) for half in range(2)] for comp in range(2)]
    for seg in range(WINDOW // FINE):
        tap_of = jnp.zeros((FINE, 128), jnp.float32)
        for q in range(BLOCK):
            if 0 <= seg - q < TAPS:
                tap_of = jnp.where(frame == q, spread[seg - q], tap_of)
        for comp in range(2):
            for half in range(2):
                weight = tap_of * columns[comp][half]
                high = weight.astype(jnp.bfloat16)
                at = (pl.ds(comp * WINDOW + seg * FINE, FINE), pl.ds(half * 128, 128))
                w_hi[at] = high
                w_lo[at] = (weight - high.astype(jnp.float32)).astype(jnp.bfloat16)

    def starts(tile):
        if tile < 2:
            base = (c if tile == 0 else 1 - c) * OWN
            return [base + j * BLOCK * FINE for j in range(8)]
        return [core * OWN + j * BLOCK * FINE for core in range(2) for j in range(8, 12)]

    def spectra(coarses, tiles):
        rows = []
        for coarse in coarses:
            for tile in tiles:
                for start in starts(tile):
                    at = pl.ds(pl.multiple_of(start, 128), WINDOW)
                    rows.append(
                        jnp.concatenate([vbuf[0, coarse, :, at], vbuf[1, coarse, :, at]], axis=1)
                    )
        left = jnp.concatenate(rows, axis=0)
        both = jnp.dot(left, w_hi[...], preferred_element_type=jnp.float32)
        both = both + jnp.dot(left, w_lo[...], preferred_element_type=jnp.float32)
        row = 0
        for coarse in coarses:
            for tile in tiles:
                for half in range(2):
                    turned = swap_groups(
                        [
                            both[row + 16 * j : row + 16 * j + 16, 128 * half : 128 * half + 128]
                            for j in range(8)
                        ]
                    )
                    for fine in range(8):
                        sbuf[coarse, half * 8 + fine, :, pl.ds(tile * 128, 128)] = turned[fine].astype(
                            jnp.bfloat16
                        )
                row += 128

    def send(coarse, place, to_zh, lo, size):
        to_s = coarse * 8 + place
        mine = jnp.logical_and(to_s == s, to_zh == zh)
        part = pl.ds(lo, size)
        source = sbuf.at[coarse, 2 * place + to_zh, :, part]
        target = owned.at[zh * 64 + s, :, part]

        @pl.when(jnp.logical_not(mine))
        def _():
            pltpu.make_async_remote_copy(
                source, target, send_sem, recv_sem,
                device_id=(to_s, to_zh * 2 + c), device_id_type=MESH,
            ).start()

        @pl.when(mine)
        def _():
            pltpu.make_async_copy(source, target, own_sem).start()

    def send_first(coarse, to_zh):
        @pl.loop(0, 8, unroll=8)
        def _(place):
            send(coarse, place, to_zh, 0, 128)

    def first(part):
        coarses = [coarse_at(4 * part + i) for i in range(4)]
        for coarse in coarses:
            own_load(coarse).wait()
        spectra(coarses, (0,))

    first(0)

    @pl.when(zh == 0)
    def _():
        pl.semaphore_wait(barrier, 64)
        start_siblings()
        pl.semaphore_wait(b_in, 1)
        pl.semaphore_signal(a_ready, 1, device_id=opposite, device_id_type=MESH)
        pl.semaphore_signal(b_ready.at[s // 8], 1)

        @pl.loop(1, 64, unroll=9)
        def _(i):
            pl.semaphore_signal(
                b_ready.at[s // 8], 1, device_id=((s + i) % 64, c), device_id_type=MESH
            )

    @pl.when(zh == 1)
    def _():
        pl.semaphore_wait(a_ready, 1)

    @pl.loop(0, 4)
    def _(k):
        send_first(coarse_at(k), 0)

    first(1)

    @pl.loop(4, COARSE)
    def _(k):
        send_first(coarse_at(k), 0)

    @pl.loop(0, COARSE)
    def _(k):
        coarse = coarse_at(k)

        @pl.when(zh == 0)
        def _():
            pl.semaphore_wait(b_ready.at[coarse], 8)
            pl.semaphore_signal(bb_ready.at[coarse], 1, device_id=(s, 2 + c), device_id_type=MESH)

        @pl.when(zh == 1)
        def _():
            pl.semaphore_wait(bb_ready.at[coarse], 1)

        send_first(coarse, 1)

    @pl.loop(0, COARSE // 2)
    def _(pair):
        coarses = [coarse_at(2 * pair), coarse_at(2 * pair + 1)]
        for coarse in coarses:
            to_sibling(coarse).wait_recv()

            @pl.when(zh == 0)
            def _():
                rim_here = vbuf.at[:, coarse, :, rim_at]
                pltpu.make_async_copy(rim_here, rim_here, rim_recv.at[coarse]).wait()

                @pl.when(c == 0)
                def _():
                    pltpu.make_async_remote_copy(
                        rim_here, rim_here, rim_send, rim_recv.at[coarse],
                        device_id=(s, 1), device_id_type=MESH,
                    ).start()

        spectra(coarses, (1, 2))

        for coarse in coarses:
            @pl.loop(0, 8, unroll=8)
            def _(place):
                send(coarse, place, 0, 128, 256)

    @pl.loop(0, COARSE)
    def _(k):
        coarse = coarse_at(k)

        @pl.loop(0, 8, unroll=8)
        def _(place):
            send(coarse, place, 1, 128, 256)

    pltpu.make_async_copy(volts, volts, sib_send).wait()

    @pl.when(c == 0)
    def _():
        rim_all = vbuf.at[:, :, :, rim_at]
        pltpu.make_async_copy(rim_all, rim_all, rim_send).wait()

    pltpu.make_async_copy(sbuf.at[0, 0], sbuf.at[0, 0], own_sem).wait()
    sent = owned.at[pl.ds(0, 127)]
    pltpu.make_async_copy(sent, sent, send_sem).wait()
    pltpu.make_async_copy(sent, sent, recv_sem).wait()


def exchange(voltages, taps):
    vmem = pl.BlockSpec(memory_space=pltpu.VMEM)
    return pl.pallas_call(
        exchange_kernel,
        out_shape=jax.ShapeDtypeStruct((128, INPUTS, CHUNK), jnp.bfloat16),
        in_specs=[pl.BlockSpec(memory_space=pl.ANY), vmem],
        out_specs=vmem,
        scratch_shapes=[
            pltpu.VMEM((2, COARSE, INPUTS, ALL + RIM), jnp.bfloat16),
            pltpu.VMEM((COARSE, HALF, INPUTS, CHUNK), jnp.bfloat16),
            pltpu.VMEM((K, 256), jnp.bfloat16),
            pltpu.VMEM((K, 256), jnp.bfloat16),
            pltpu.SemaphoreType.DMA((COARSE,)),
            pltpu.SemaphoreType.DMA,
            pltpu.SemaphoreType.DMA((COARSE,)),
            pltpu.SemaphoreType.DMA,
            pltpu.SemaphoreType.DMA((COARSE,)),
            pltpu.SemaphoreType.DMA,
            pltpu.SemaphoreType.DMA,
            pltpu.SemaphoreType.DMA,
            pltpu.SemaphoreType.REGULAR,
            pltpu.SemaphoreType.REGULAR,
            pltpu.SemaphoreType.REGULAR((COARSE,)),
            pltpu.SemaphoreType.REGULAR((COARSE,)),
        ],
        compiler_params=pltpu.CompilerParams(
            collective_id=0, has_side_effects=True, vmem_limit_bytes=VMEM_LIMIT
        ),
        name="exchange",
    )(voltages, taps)


def gram_kernel(factor, data, out, buf, sems):
    lane = lax.broadcasted_iota(jnp.int32, (COLUMNS, 128), 1)
    sign = jnp.where(lane < 64, -1.0, 1.0)
    left = jnp.concatenate([data[0], data[1]], axis=1)
    copies = []
    for i in range(1024 // COLUMNS):
        at = pl.ds(i * COLUMNS, COLUMNS)
        plain, turned = [], []
        for zh in range(2):
            plain.append(data[zh, at, :])
            for tile in range(CHUNK // 128):
                part = data[zh, at, pl.ds(tile * 128, 128)].astype(jnp.float32)
                turned.append((pltpu.roll(part, 64, 1) * sign).astype(jnp.bfloat16))
        right = jnp.concatenate(
            [jnp.concatenate(plain, axis=1), jnp.concatenate(turned, axis=1)], axis=0
        )
        both = lax.dot_general(
            left, right, (((1,), (1,)), ((), ())), preferred_element_type=jnp.float32
        )
        buf[i, 0] = both[:, :COLUMNS] * factor
        buf[i, 1] = both[:, COLUMNS:] * factor
        copies.append(pltpu.make_async_copy(buf.at[i], out.at[:, :, at], sems.at[i]))
        copies[i].start()
    for copy in copies:
        copy.wait()


def gram(data, factor):
    return pl.pallas_call(
        functools.partial(gram_kernel, factor),
        out_shape=jax.ShapeDtypeStruct((2, 1024, 1024), jnp.float32),
        in_specs=[pl.BlockSpec(memory_space=pltpu.VMEM)],
        out_specs=pl.BlockSpec(memory_space=pl.ANY),
        scratch_shapes=[
            pltpu.VMEM((1024 // COLUMNS, 2, 1024, COLUMNS), jnp.float32),
            pltpu.SemaphoreType.DMA((1024 // COLUMNS,)),
        ],
        compiler_params=pltpu.CompilerParams(vmem_limit_bytes=48 << 20),
        name="gram",
    )(data)


def on_device(voltages, filter_taps):
    owned = exchange(voltages, filter_taps)
    return gram(owned.reshape(2, 1024, CHUNK), 1.0 / (4 * FRAMES))[None]


def solution(mesh):
    return jax.shard_map(
        on_device,
        mesh=mesh,
        in_specs=(P(None, None, "stn", "tm"), P()),
        out_specs=P(("stn", "tm"), None, None, None),
        check_vma=False,
    )
```
